32 devices in a mesh: cplx: 2 (over y), row: 4 (over x, core), col: 4 (over z).
Axes of the slice: x: 2, y: 2, z: 4, core: 2. Of those that a mesh axis runs over, the one named last changes fastest.
Arguments:
- pair_rep: bfloat16 [128, 64, 128], P(('cplx', 'row'), 'col'), parts along dimension 0, may hold values from -6 to 6
- pair_mask: int32 [128, 64], P(('cplx', 'row'), 'col'), parts along dimension 0, may hold values from 0 to 1, as said below
- norm_gain: float32 [128], replicated, may hold values from 0.5 to 1.5
- norm_bias: float32 [128], replicated, may hold values from -3 to 3
- proj_weight: bfloat16 [128, 640], replicated, may hold values from -0.5 to 0.5
- out_gain: float32 [128], replicated, may hold values from 0.5 to 1.5
- out_bias: float32 [128], replicated, may hold values from -3 to 3
- out_weight: bfloat16 [128, 128], replicated, may hold values from -0.5 to 0.5
Outputs:
- update: bfloat16 [128, 64, 128], P(('cplx', 'row', 'col')), parts along dimension 0
The draws below stay inside these ranges and needn't reach their ends.
There are 2 independent parts, one for each index of `cplx`. The reference program is written for one: setup_inputs(seed, part) draws one part's arguments, and reference() takes and returns one part's arrays. A program takes and returns all parts, laid end to end along the dimension named above; an argument that names none is the same for every part. Nothing has to cross between parts.
Inputs may be any that keep to these rules, and one draw needn't show every extreme that they name: pair_mask[i, j] = v[i] v[j] for a 0/1 validity v of the tokens.
All inputs are finite; a program needn't handle non-finite values.
Results may differ from the reference program's by a relative error of at most 0.0085.
Values may be sent and summed in bfloat16 or wider, within the bound.
A program may use at most 128 MiB of HBM per device.

```python
import jax
import jax.numpy as jnp
from jax import lax

C = 128
NTOK = 64


def draw_pair_mask(key, part):
    key = jax.random.fold_in(key, 11)
    first_key, second_key = jax.random.split(key)
    length = jax.random.randint(first_key, (), NTOK * 3 // 4, NTOK + 1)
    keeper = jax.random.randint(second_key, (NTOK,), 0, 16) != 0
    position = jnp.arange(NTOK)
    validity = ((position < length) & keeper).astype(jnp.int32)
    return validity[:, None] * validity[None, :]


def shard_levels(key, extent, shards, least, high):
    level, own = 1.0, jax.random.fold_in(key, 6)
    for dim, shards_of in shards:
        draws = jnp.exp(jax.random.uniform(jax.random.fold_in(own, dim), (shards_of,), jnp.float32, least / len(shards), high / len(shards)))
        level = level * jnp.repeat(draws, extent[dim] // shards_of).reshape([-1 if axis == dim else 1 for axis in range(len(extent))])
    return level


def noise(stream_key, dims, scale, bound, shards=(), kind=jnp.bfloat16):
    drawn = scale * jax.random.normal(stream_key, dims, jnp.float32)
    if shards:
        drawn = drawn * shard_levels(stream_key, dims, shards, -0.22, 0.18)
    return jnp.clip(drawn, -bound, bound).astype(kind)


def setup_inputs(seed: int = 0, part: int = 0) -> dict:
    key_list = jax.random.split(jax.random.key(seed), 9)
    part_splits = jax.random.split(jax.random.fold_in(key_list[8], part), 9)
    return {
        "pair_rep": noise(part_splits[0], (NTOK, NTOK, C), 1.0, 6.0, ((0, 4), (1, 4))),
        "pair_mask": draw_pair_mask(jax.random.fold_in(jax.random.fold_in(key_list[8], part), 71), part),
        "norm_gain": jnp.clip(jax.random.uniform(key_list[2], (C,), jnp.float32, 0.5, 1.5), 0.5, 1.5),
        "norm_bias": noise(key_list[3], (C,), 0.5, 3.0, (), jnp.float32),
        "proj_weight": noise(key_list[4], (C, 5 * C), C ** -0.5, 0.5),
        "out_gain": jnp.clip(jax.random.uniform(key_list[5], (C,), jnp.float32, 0.5, 1.5), 0.5, 1.5),
        "out_bias": noise(key_list[6], (C,), 0.5, 3.0, (), jnp.float32),
        "out_weight": noise(key_list[7], (C, C), C ** -0.5, 0.5),
    }


def normalize(values, scale_gain, shift_bias):
    average = lax.optimization_barrier(jnp.mean(values, axis=-1, keepdims=True))
    centered = values - average
    variance = lax.optimization_barrier(jnp.mean(centered * centered, axis=-1, keepdims=True))
    return centered * lax.rsqrt(variance + 1e-05) * scale_gain + shift_bias

def reference(pair_rep, pair_mask, norm_gain, norm_bias, proj_weight, out_gain, out_bias, out_weight):
    channels = pair_rep.shape[2]
    blocks = 8

    def prepare(inputs):
        pair_block, mask_block = inputs
        normed = normalize(pair_block.astype(jnp.float32), norm_gain, norm_bias).astype(jnp.bfloat16)
        projected = jnp.dot(normed.reshape(-1, channels), proj_weight, preferred_element_type=jnp.float32)
        projected = projected.reshape(pair_block.shape[0], pair_block.shape[1], 5 * channels)
        validity = mask_block.astype(jnp.float32)[:, :, None]
        left_side = (jax.nn.sigmoid(projected[:, :, :channels]) * projected[:, :, channels:2 * channels] * validity).astype(jnp.bfloat16)
        right_side = (jax.nn.sigmoid(projected[:, :, 2 * channels:3 * channels]) * projected[:, :, 3 * channels:4 * channels] * validity).astype(jnp.bfloat16)
        gating = jax.nn.sigmoid(projected[:, :, 4 * channels:]).astype(jnp.bfloat16)
        return (left_side, right_side, gating)
    left_side, right_side, gating = lax.map(prepare, (pair_rep.reshape(blocks, -1, NTOK, channels), pair_mask.reshape(blocks, -1, NTOK)))
    right_wide = right_side.reshape(NTOK, NTOK, channels).astype(jnp.float32)

    def combine(inputs):
        left_block, gate_block = inputs
        mixed_sum = jnp.einsum('ikc,jkc->ijc', left_block.astype(jnp.float32), right_wide)
        normed_out = normalize(mixed_sum, out_gain, out_bias).astype(jnp.bfloat16)
        lifted = jnp.dot(normed_out.reshape(-1, channels), out_weight, preferred_element_type=jnp.float32)
        lifted = lifted.reshape(mixed_sum.shape)
        return (gate_block.astype(jnp.float32) * lifted).astype(jnp.bfloat16)
    update = lax.map(combine, (left_side, gating))
    return update.reshape(NTOK, NTOK, channels)
```

```python
import functools

import jax
import jax.numpy as jnp
from jax import lax
from jax.experimental import pallas as pl
from jax.experimental.pallas import tpu as pltpu
from jax.sharding import PartitionSpec as P

MESH = pl.DeviceIdType.MESH
F32, BF16 = jnp.float32, jnp.bfloat16


def normalize(values, scale_gain, shift_bias):
    average = jnp.mean(values, axis=-1, keepdims=True)
    centered = values - average
    variance = jnp.mean(centered * centered, axis=-1, keepdims=True)
    return centered * lax.rsqrt(variance + 1e-05) * scale_gain + shift_bias


def finish(mixed_sum, gating, out_gain, out_bias, out_weight):
    channels = mixed_sum.shape[2]
    normed_out = normalize(mixed_sum, out_gain, out_bias).astype(BF16)
    lifted = jnp.dot(
        normed_out.reshape(-1, channels), out_weight, preferred_element_type=F32
    )
    lifted = lifted.reshape(mixed_sum.shape)
    return (gating.astype(F32) * lifted).astype(BF16)


def general_form(
    pair_rep, pair_mask, norm_gain, norm_bias, proj_weight, out_gain, out_bias, out_weight
):
    rows, cols, channels = pair_rep.shape
    normed = normalize(pair_rep.astype(F32), norm_gain, norm_bias).astype(BF16)
    projected = jnp.dot(normed.reshape(-1, channels), proj_weight, preferred_element_type=F32)
    projected = projected.reshape(rows, cols, 5 * channels)
    validity = pair_mask.astype(F32)[:, :, None]
    p = [projected[:, :, n * channels : (n + 1) * channels] for n in range(5)]
    left_side = (jax.nn.sigmoid(p[0]) * p[1] * validity).astype(BF16)
    right_side = (jax.nn.sigmoid(p[2]) * p[3] * validity).astype(BF16)
    gating = jax.nn.sigmoid(p[4]).astype(BF16)
    partial_value = jnp.einsum(
        "ikc,jkc->ijc",
        left_side,
        lax.all_gather(right_side, "row", axis=0, tiled=True),
        preferred_element_type=F32,
    )
    mixed_sum = lax.psum_scatter(partial_value, "col", scatter_dimension=1, tiled=True)
    update = finish(mixed_sum, gating, out_gain, out_bias, out_weight)
    return lax.all_to_all(update, "col", split_axis=0, concat_axis=1, tiled=True)


def kernel(
    sizes,
    x_hbm, mask_hbm, gain_hbm, bias_hbm, w_hbm, ogain_hbm, obias_hbm, ow_hbm,
    out_ref,
    x_v, mask_v, gain_v, bias_v, w_v, ogain_v, obias_v, ow_v,
    right_f, left_f, right_b, x_g, gate, part_s, part_r, part_own,
    in_sem, right_ss, right_rs, x_ss, x_rs, part_ss, part_rs,
):
    R, S, ti, tk, C = sizes
    so = ti // S
    row, col = lax.axis_index("row"), lax.axis_index("col")

    barrier = pltpu.get_barrier_semaphore()
    for off in range(1, R):
        pl.semaphore_signal(barrier, inc=1, device_id={"row": row ^ off}, device_id_type=MESH)
    for off in range(1, S):
        pl.semaphore_signal(barrier, inc=1, device_id={"col": col ^ off}, device_id_type=MESH)

    loads = [
        pltpu.make_async_copy(src, dst, in_sem.at[n])
        for n, (src, dst) in enumerate(
            [
                (x_hbm, x_v), (mask_hbm, mask_v), (gain_hbm, gain_v), (bias_hbm, bias_v),
                (w_hbm, w_v), (ogain_hbm, ogain_v), (obias_hbm, obias_v), (ow_hbm, ow_v),
                (x_hbm.at[pl.ds(col * so, so)], x_g.at[0]),
            ]
        )
    ]
    for load in loads:
        load.start()
    for load in loads:
        load.wait()

    gain, bias = gain_v[...].reshape(1, C), bias_v[...].reshape(1, C)
    validity = mask_v[...].astype(F32)[:, :, None]
    step = max(1, 64 // tk)
    for i0 in range(0, ti, step):
        x = x_v[i0 : i0 + step].astype(F32).reshape(step * tk, C)
        normed = normalize(x, gain, bias).astype(BF16)
        p = jnp.dot(normed, w_v[:, : 4 * C], preferred_element_type=F32)
        valid = validity[i0 : i0 + step].reshape(step * tk, 1)
        left = jax.nn.sigmoid(p[:, :C]) * p[:, C : 2 * C] * valid
        right = jax.nn.sigmoid(p[:, 2 * C : 3 * C]) * p[:, 3 * C :] * valid
        left_f[i0 * tk : (i0 + step) * tk] = left.astype(BF16).astype(F32)
        right_f[i0 * tk : (i0 + step) * tk] = right
    for k in range(tk):
        right_b[0, k] = right_f[pl.ds(k, ti, stride=tk), :].astype(BF16)

    pl.semaphore_wait(barrier, R + S - 2)

    right_copies = {
        off: pltpu.make_async_remote_copy(
            src_ref=right_b.at[0], dst_ref=right_b.at[off],
            send_sem=right_ss.at[off], recv_sem=right_rs.at[off],
            device_id={"row": row ^ off}, device_id_type=MESH,
        )
        for off in range(1, R)
    }
    x_copies = {
        off: pltpu.make_async_remote_copy(
            src_ref=x_hbm.at[pl.ds((col ^ off) * so, so)], dst_ref=x_g.at[off],
            send_sem=x_ss.at[off], recv_sem=x_rs.at[off],
            device_id={"col": col ^ off}, device_id_type=MESH,
        )
        for off in range(1, S)
    }
    for off in range(R - 1, 0, -1):
        right_copies[off].start()
    for off in range(S - 1, 0, -1):
        x_copies[off].start()

    part_copies = {
        (off, s): pltpu.make_async_remote_copy(
            src_ref=part_s.at[off, s], dst_ref=part_r.at[off, s],
            send_sem=part_ss.at[off, s], recv_sem=part_rs.at[off, s],
            device_id={"col": col ^ s}, device_id_type=MESH,
        )
        for off in range(R)
        for s in range(1, S)
    }

    def mix(off):
        right = [right_b[off, k].astype(F32) for k in range(tk)]
        for s in list(range(S - 1, -1, -1)):
            base = (col ^ s) * (so * tk)

            def one_row(ii, carry):
                at = base + ii * tk
                sums = [None, None]
                for k in range(tk):
                    term = left_f[pl.ds(at + k, 1), :] * right[k]
                    sums[k % 2] = term if sums[k % 2] is None else sums[k % 2] + term
                total = sums[0] + sums[1]
                if s:
                    part_s[off, s, ii] = total.astype(BF16)
                else:
                    part_own[off, ii] = total
                return carry

            lax.fori_loop(0, so, one_row, 0, unroll=True)
            if s:
                part_copies[off, s].start()

    def gates():
        for off in range(1, S):
            x_copies[off].wait_recv()
        for off in range(S):
            x = x_g[off].astype(F32).reshape(so * tk, C)
            normed = normalize(x, gain, bias).astype(BF16)
            p = jnp.dot(normed, w_v[:, 4 * C :], preferred_element_type=F32)
            g = jax.nn.sigmoid(p).astype(BF16).astype(F32)
            gate[:, pl.ds(pl.multiple_of((col ^ off) * tk, tk), tk), :] = g.reshape(so, tk, C)

    def close(off):
        total = part_own[off]
        for s in range(1, S):
            part_copies[off, s].wait_recv()
            total = total + part_r[off, s].astype(F32)
        total = total.reshape(so * ti, C)
        ogain, obias = ogain_v[...].reshape(1, C), obias_v[...].reshape(1, C)
        normed_out = normalize(total, ogain, obias).astype(BF16)
        lifted = jnp.dot(normed_out, ow_v[...], preferred_element_type=F32)
        at = pl.ds(pl.multiple_of((row ^ off) * ti, ti), ti)
        out_ref[:, at, :] = (gate[:, at, :] * lifted.reshape(so, ti, C)).astype(BF16)

    mix(0)
    for off in range(1, R):
        right_copies[off].wait_recv()
        mix(off)
        if off == 1:
            gates()
    if R == 1:
        gates()
    for off in range(R):
        close(off)

    for copies in (right_copies, x_copies, part_copies):
        for copy in copies.values():
            copy.wait_send()


def kernel_form(R, S, *arguments):
    pair_rep = arguments[0]
    ti, tk, C = pair_rep.shape
    so = ti // S
    vmem, dma = pltpu.VMEM, pltpu.SemaphoreType.DMA
    return pl.pallas_call(
        functools.partial(kernel, (R, S, ti, tk, C)),
        out_shape=jax.ShapeDtypeStruct((so, R * ti, C), BF16),
        in_specs=[pl.BlockSpec(memory_space=pl.ANY)] * 8,
        out_specs=pl.BlockSpec(memory_space=pltpu.VMEM),
        scratch_shapes=[vmem(a.shape, a.dtype) for a in arguments]
        + [
            vmem((ti * tk, C), F32),
            vmem((ti * tk, C), F32),
            vmem((R, tk, ti, C), BF16),
            vmem((S, so, tk, C), BF16),
            vmem((so, S * tk, C), F32),
            vmem((R, S, so, ti, C), BF16),
            vmem((R, S, so, ti, C), BF16),
            vmem((R, so, ti, C), F32),
            dma((9,)), dma((R,)), dma((R,)), dma((S,)), dma((S,)), dma((R, S)), dma((R, S)),
        ],
        compiler_params=pltpu.CompilerParams(
            collective_id=0, has_side_effects=True, vmem_limit_bytes=24 * 2**20
        ),
    )(*arguments)


def solution(mesh):
    R, S = mesh.shape["row"], mesh.shape["col"]

    def on_device(*arguments):
        ti, tk, C = arguments[0].shape
        small = (
            R in (2, 4) and S in (2, 4) and R * ti == S * tk and C == 128
            and ti == 16 and tk == 16
        )
        if small:
            return kernel_form(R, S, *arguments)
        return general_form(*arguments)

    return jax.shard_map(
        on_device,
        mesh=mesh,
        in_specs=(P(("cplx", "row"), "col", None), P(("cplx", "row"), "col"))
        + (P(),) * 6,
        out_specs=P(("cplx", "row", "col"), None, None),
        check_vma=False,
    )
```

```python
import functools

import jax
import jax.numpy as jnp
from jax import lax
from jax.experimental import pallas as pl
from jax.experimental.pallas import tpu as pltpu
from jax.sharding import PartitionSpec as P

MESH = pl.DeviceIdType.MESH
F32, BF16 = jnp.float32, jnp.bfloat16


def normalize(values, scale_gain, shift_bias):
    average = jnp.mean(values, axis=-1, keepdims=True)
    centered = values - average
    variance = jnp.mean(centered * centered, axis=-1, keepdims=True)
    return centered * lax.rsqrt(variance + 1e-05) * scale_gain + shift_bias


def finish(mixed_sum, gating, out_gain, out_bias, out_weight):
    channels = mixed_sum.shape[2]
    normed_out = normalize(mixed_sum, out_gain, out_bias).astype(BF16)
    lifted = jnp.dot(
        normed_out.reshape(-1, channels), out_weight, preferred_element_type=F32
    )
    lifted = lifted.reshape(mixed_sum.shape)
    return (gating.astype(F32) * lifted).astype(BF16)


def general_form(
    pair_rep, pair_mask, norm_gain, norm_bias, proj_weight, out_gain, out_bias, out_weight
):
    rows, cols, channels = pair_rep.shape
    normed = normalize(pair_rep.astype(F32), norm_gain, norm_bias).astype(BF16)
    projected = jnp.dot(normed.reshape(-1, channels), proj_weight, preferred_element_type=F32)
    projected = projected.reshape(rows, cols, 5 * channels)
    validity = pair_mask.astype(F32)[:, :, None]
    p = [projected[:, :, n * channels : (n + 1) * channels] for n in range(5)]
    left_side = (jax.nn.sigmoid(p[0]) * p[1] * validity).astype(BF16)
    right_side = (jax.nn.sigmoid(p[2]) * p[3] * validity).astype(BF16)
    gating = jax.nn.sigmoid(p[4]).astype(BF16)
    partial_value = jnp.einsum(
        "ikc,jkc->ijc",
        left_side,
        lax.all_gather(right_side, "row", axis=0, tiled=True),
        preferred_element_type=F32,
    )
    mixed_sum = lax.psum_scatter(partial_value, "col", scatter_dimension=1, tiled=True)
    update = finish(mixed_sum, gating, out_gain, out_bias, out_weight)
    return lax.all_to_all(update, "col", split_axis=0, concat_axis=1, tiled=True)


def kernel(
    sizes,
    x_hbm, mask_hbm, gain_hbm, bias_hbm, w_hbm, ogain_hbm, obias_hbm, ow_hbm,
    out_ref,
    x_v, mask_v, gain_v, bias_v, w_v, ogain_v, obias_v, ow_v,
    right_f, left_f, right_b, x_g, gate, part_s, part_r, part_own,
    in_sem, right_ss, right_rs, x_ss, x_rs, part_ss, part_rs,
):
    R, S, ti, tk, C = sizes
    so = ti // S
    row, col = lax.axis_index("row"), lax.axis_index("col")

    barrier = pltpu.get_barrier_semaphore()
    for off in range(1, R):
        pl.semaphore_signal(barrier, inc=1, device_id={"row": row ^ off}, device_id_type=MESH)
    for off in range(1, S):
        pl.semaphore_signal(barrier, inc=1, device_id={"col": col ^ off}, device_id_type=MESH)

    loads = [
        pltpu.make_async_copy(src, dst, in_sem.at[n])
        for n, (src, dst) in enumerate(
            [
                (x_hbm, x_v), (mask_hbm, mask_v), (gain_hbm, gain_v), (bias_hbm, bias_v),
                (w_hbm, w_v), (ogain_hbm, ogain_v), (obias_hbm, obias_v), (ow_hbm, ow_v),
                (x_hbm.at[pl.ds(col * so, so)], x_g.at[0]),
            ]
        )
    ]
    for load in loads:
        load.start()
    pl.semaphore_wait(barrier, R + S - 2)
    x_copies = {
        off: pltpu.make_async_remote_copy(
            src_ref=x_hbm.at[pl.ds((col ^ off) * so, so)], dst_ref=x_g.at[off],
            send_sem=x_ss.at[off], recv_sem=x_rs.at[off],
            device_id={"col": col ^ off}, device_id_type=MESH,
        )
        for off in range(1, S)
    }
    for off in range(S - 1, 0, -1):
        x_copies[off].start()
    for load in loads:
        load.wait()

    gain, bias = gain_v[...].reshape(1, C), bias_v[...].reshape(1, C)
    validity = mask_v[...].astype(F32)[:, :, None]
    step = max(1, 64 // tk)
    for i0 in range(0, ti, step):
        x = x_v[i0 : i0 + step].astype(F32).reshape(step * tk, C)
        normed = normalize(x, gain, bias).astype(BF16)
        p = jnp.dot(normed, w_v[:, : 4 * C], preferred_element_type=F32)
        valid = validity[i0 : i0 + step].reshape(step * tk, 1)
        left = jax.nn.sigmoid(p[:, :C]) * p[:, C : 2 * C] * valid
        right = jax.nn.sigmoid(p[:, 2 * C : 3 * C]) * p[:, 3 * C :] * valid
        left_f[i0 * tk : (i0 + step) * tk] = left.astype(BF16).astype(F32)
        right_f[i0 * tk : (i0 + step) * tk] = right
    for k in range(tk):
        right_b[0, k] = right_f[pl.ds(k, ti, stride=tk), :].astype(BF16)

    right_copies = {
        off: pltpu.make_async_remote_copy(
            src_ref=right_b.at[0], dst_ref=right_b.at[off],
            send_sem=right_ss.at[off], recv_sem=right_rs.at[off],
            device_id={"row": row ^ off}, device_id_type=MESH,
        )
        for off in range(1, R)
    }
    for off in range(R - 1, 0, -1):
        right_copies[off].start()

    part_copies = {
        (off, s): pltpu.make_async_remote_copy(
            src_ref=part_s.at[off, s], dst_ref=part_r.at[off, s],
            send_sem=part_ss.at[off, s], recv_sem=part_rs.at[off, s],
            device_id={"col": col ^ s}, device_id_type=MESH,
        )
        for off in range(R)
        for s in range(1, S)
    }

    def mix(off):
        right = [right_b[off, k].astype(F32) for k in range(tk)]
        for s in list(range(S - 1, -1, -1)):
            base = (col ^ s) * (so * tk)

            def one_row(ii, carry):
                at = base + ii * tk
                sums = [None, None]
                for k in range(tk):
                    term = left_f[pl.ds(at + k, 1), :] * right[k]
                    sums[k % 2] = term if sums[k % 2] is None else sums[k % 2] + term
                total = sums[0] + sums[1]
                if s:
                    part_s[off, s, ii] = total.astype(BF16)
                else:
                    part_own[off, ii] = total
                return carry

            lax.fori_loop(0, so, one_row, 0, unroll=True)
            if s:
                part_copies[off, s].start()

    def gates():
        for off in range(1, S):
            x_copies[off].wait_recv()
        for off in range(S):
            x = x_g[off].astype(F32).reshape(so * tk, C)
            normed = normalize(x, gain, bias).astype(BF16)
            p = jnp.dot(normed, w_v[:, 4 * C :], preferred_element_type=F32)
            g = jax.nn.sigmoid(p).astype(BF16).astype(F32)
            gate[:, pl.ds(pl.multiple_of((col ^ off) * tk, tk), tk), :] = g.reshape(so, tk, C)

    def close(off):
        total = part_own[off]
        for s in range(1, S):
            part_copies[off, s].wait_recv()
            total = total + part_r[off, s].astype(F32)
        total = total.reshape(so * ti, C)
        ogain, obias = ogain_v[...].reshape(1, C), obias_v[...].reshape(1, C)
        normed_out = normalize(total, ogain, obias).astype(BF16)
        lifted = jnp.dot(normed_out, ow_v[...], preferred_element_type=F32)
        at = pl.ds(pl.multiple_of((row ^ off) * ti, ti), ti)
        out_ref[:, at, :] = (gate[:, at, :] * lifted.reshape(so, ti, C)).astype(BF16)

    mix(0)
    for off in range(1, R):
        right_copies[off].wait_recv()
        mix(off)
        if off == 1:
            gates()
    if R == 1:
        gates()
    for off in range(R):
        close(off)

    for copies in (right_copies, x_copies, part_copies):
        for copy in copies.values():
            copy.wait_send()


def kernel_form(R, S, *arguments):
    pair_rep = arguments[0]
    ti, tk, C = pair_rep.shape
    so = ti // S
    vmem, dma = pltpu.VMEM, pltpu.SemaphoreType.DMA
    return pl.pallas_call(
        functools.partial(kernel, (R, S, ti, tk, C)),
        out_shape=jax.ShapeDtypeStruct((so, R * ti, C), BF16),
        in_specs=[pl.BlockSpec(memory_space=pl.ANY)] * 8,
        out_specs=pl.BlockSpec(memory_space=pltpu.VMEM),
        scratch_shapes=[vmem(a.shape, a.dtype) for a in arguments]
        + [
            vmem((ti * tk, C), F32),
            vmem((ti * tk, C), F32),
            vmem((R, tk, ti, C), BF16),
            vmem((S, so, tk, C), BF16),
            vmem((so, S * tk, C), F32),
            vmem((R, S, so, ti, C), BF16),
            vmem((R, S, so, ti, C), BF16),
            vmem((R, so, ti, C), F32),
            dma((9,)), dma((R,)), dma((R,)), dma((S,)), dma((S,)), dma((R, S)), dma((R, S)),
        ],
        compiler_params=pltpu.CompilerParams(
            collective_id=0, has_side_effects=True, vmem_limit_bytes=56 * 2**20
        ),
    )(*arguments)


def solution(mesh):
    R, S = mesh.shape["row"], mesh.shape["col"]

    def on_device(*arguments):
        ti, tk, C = arguments[0].shape
        small = (
            R in (2, 4) and S in (2, 4) and R * ti == S * tk and C == 128
            and ti == 16 and tk == 16
        )
        if small:
            return kernel_form(R, S, *arguments)
        return general_form(*arguments)

    return jax.shard_map(
        on_device,
        mesh=mesh,
        in_specs=(P(("cplx", "row"), "col", None), P(("cplx", "row"), "col"))
        + (P(),) * 6,
        out_specs=P(("cplx", "row", "col"), None, None),
        check_vma=False,
    )
```

```python
import functools

import jax
import jax.numpy as jnp
from jax import lax
from jax.experimental import pallas as pl
from jax.experimental.pallas import tpu as pltpu
from jax.sharding import PartitionSpec as P

MESH = pl.DeviceIdType.MESH
F32, BF16 = jnp.float32, jnp.bfloat16


def normalize(values, scale_gain, shift_bias):
    average = jnp.mean(values, axis=-1, keepdims=True)
    centered = values - average
    variance = jnp.mean(centered * centered, axis=-1, keepdims=True)
    return centered * lax.rsqrt(variance + 1e-05) * scale_gain + shift_bias


def finish(mixed_sum, gating, out_gain, out_bias, out_weight):
    channels = mixed_sum.shape[2]
    normed_out = normalize(mixed_sum, out_gain, out_bias).astype(BF16)
    lifted = jnp.dot(
        normed_out.reshape(-1, channels), out_weight, preferred_element_type=F32
    )
    lifted = lifted.reshape(mixed_sum.shape)
    return (gating.astype(F32) * lifted).astype(BF16)


def general_form(
    pair_rep, pair_mask, norm_gain, norm_bias, proj_weight, out_gain, out_bias, out_weight
):
    rows, cols, channels = pair_rep.shape
    normed = normalize(pair_rep.astype(F32), norm_gain, norm_bias).astype(BF16)
    projected = jnp.dot(normed.reshape(-1, channels), proj_weight, preferred_element_type=F32)
    projected = projected.reshape(rows, cols, 5 * channels)
    validity = pair_mask.astype(F32)[:, :, None]
    p = [projected[:, :, n * channels : (n + 1) * channels] for n in range(5)]
    left_side = (jax.nn.sigmoid(p[0]) * p[1] * validity).astype(BF16)
    right_side = (jax.nn.sigmoid(p[2]) * p[3] * validity).astype(BF16)
    gating = jax.nn.sigmoid(p[4]).astype(BF16)
    partial_value = jnp.einsum(
        "ikc,jkc->ijc",
        left_side,
        lax.all_gather(right_side, "row", axis=0, tiled=True),
        preferred_element_type=F32,
    )
    mixed_sum = lax.psum_scatter(partial_value, "col", scatter_dimension=1, tiled=True)
    update = finish(mixed_sum, gating, out_gain, out_bias, out_weight)
    return lax.all_to_all(update, "col", split_axis=0, concat_axis=1, tiled=True)


def kernel(
    sizes,
    x_hbm, mask_hbm, gain_hbm, bias_hbm, w_hbm, ogain_hbm, obias_hbm, ow_hbm,
    out_ref,
    x_v, mask_v, gain_v, bias_v, w_v, ogain_v, obias_v, ow_v,
    right_f, left_f, right_b, x_g, gate, part_s, part_r, part_own,
    in_sem, right_ss, right_rs, x_ss, x_rs, part_ss, part_rs,
):
    R, S, ti, tk, C = sizes
    so = ti // S
    row, col = lax.axis_index("row"), lax.axis_index("col")

    barrier = pltpu.get_barrier_semaphore()
    for off in range(1, R):
        pl.semaphore_signal(barrier, inc=1, device_id={"row": row ^ off}, device_id_type=MESH)
    for off in range(1, S):
        pl.semaphore_signal(barrier, inc=1, device_id={"col": col ^ off}, device_id_type=MESH)

    loads = [
        pltpu.make_async_copy(src, dst, in_sem.at[n])
        for n, (src, dst) in enumerate(
            [
                (x_hbm, x_v), (mask_hbm, mask_v), (gain_hbm, gain_v), (bias_hbm, bias_v),
                (w_hbm, w_v), (ogain_hbm, ogain_v), (obias_hbm, obias_v), (ow_hbm, ow_v),
                (x_hbm.at[pl.ds(col * so, so)], x_g.at[0]),
            ]
        )
    ]
    for n in (4, 0, 1, 2, 3, 8, 5, 6, 7):
        loads[n].start()
    pl.semaphore_wait(barrier, R + S - 2)
    x_copies = {
        off: pltpu.make_async_remote_copy(
            src_ref=x_hbm.at[pl.ds((col ^ off) * so, so)], dst_ref=x_g.at[off],
            send_sem=x_ss.at[off], recv_sem=x_rs.at[off],
            device_id={"col": col ^ off}, device_id_type=MESH,
        )
        for off in range(1, S)
    }
    for off in range(S - 1, 0, -1):
        x_copies[off].start()
    for load in loads[:5]:
        load.wait()

    gain, bias = gain_v[...].reshape(1, C), bias_v[...].reshape(1, C)
    validity = mask_v[...].astype(F32)[:, :, None]
    step = max(1, 64 // tk)
    for i0 in range(0, ti, step):
        x = x_v[i0 : i0 + step].astype(F32).reshape(step * tk, C)
        normed = normalize(x, gain, bias).astype(BF16)
        p = jnp.dot(normed, w_v[:, : 4 * C], preferred_element_type=F32)
        valid = validity[i0 : i0 + step].reshape(step * tk, 1)
        left = jax.nn.sigmoid(p[:, :C]) * p[:, C : 2 * C] * valid
        right = jax.nn.sigmoid(p[:, 2 * C : 3 * C]) * p[:, 3 * C :] * valid
        left_f[i0 * tk : (i0 + step) * tk] = left.astype(BF16).astype(F32)
        right_f[i0 * tk : (i0 + step) * tk] = right
    for k in range(tk):
        right_b[0, k] = right_f[pl.ds(k, ti, stride=tk), :].astype(BF16)

    right_copies = {
        off: pltpu.make_async_remote_copy(
            src_ref=right_b.at[0], dst_ref=right_b.at[off],
            send_sem=right_ss.at[off], recv_sem=right_rs.at[off],
            device_id={"row": row ^ off}, device_id_type=MESH,
        )
        for off in range(1, R)
    }
    for off in range(1, R):
        right_copies[off].start()

    part_copies = {
        (off, s): pltpu.make_async_remote_copy(
            src_ref=part_s.at[off, s], dst_ref=part_r.at[off, s],
            send_sem=part_ss.at[off, s], recv_sem=part_rs.at[off, s],
            device_id={"col": col ^ s}, device_id_type=MESH,
        )
        for off in range(R)
        for s in range(1, S)
    }

    def mix(off):
        right = [right_b[off, k].astype(F32) for k in range(tk)]
        for s in list(range(S - 1, -1, -1)):
            base = (col ^ s) * (so * tk)

            def one_row(ii, carry):
                at = base + ii * tk
                sums = [None, None]
                for k in range(tk):
                    term = left_f[pl.ds(at + k, 1), :] * right[k]
                    sums[k % 2] = term if sums[k % 2] is None else sums[k % 2] + term
                total = sums[0] + sums[1]
                if s:
                    part_s[off, s, ii] = total.astype(BF16)
                else:
                    part_own[off, ii] = total
                return carry

            lax.fori_loop(0, so, one_row, 0, unroll=True)
            if s:
                part_copies[off, s].start()

    def gates():
        loads[8].wait()
        for off in range(1, S):
            x_copies[off].wait_recv()
        for off in range(S):
            x = x_g[off].astype(F32).reshape(so * tk, C)
            normed = normalize(x, gain, bias).astype(BF16)
            p = jnp.dot(normed, w_v[:, 4 * C :], preferred_element_type=F32)
            g = jax.nn.sigmoid(p).astype(BF16).astype(F32)
            gate[:, pl.ds(pl.multiple_of((col ^ off) * tk, tk), tk), :] = g.reshape(so, tk, C)

    def close(off):
        total = part_own[off]
        for s in range(1, S):
            part_copies[off, s].wait_recv()
            total = total + part_r[off, s].astype(F32)
        total = total.reshape(so * ti, C)
        ogain, obias = ogain_v[...].reshape(1, C), obias_v[...].reshape(1, C)
        normed_out = normalize(total, ogain, obias).astype(BF16)
        lifted = jnp.dot(normed_out, ow_v[...], preferred_element_type=F32)
        at = pl.ds(pl.multiple_of((row ^ off) * ti, ti), ti)
        out_ref[:, at, :] = (gate[:, at, :] * lifted.reshape(so, ti, C)).astype(BF16)

    mix(0)
    for off in range(1, R):
        right_copies[off].wait_recv()
        mix(off)
        if off == 1:
            gates()
    if R == 1:
        gates()
    for load in loads[5:8]:
        load.wait()
    for off in range(R):
        close(off)

    for copies in (right_copies, x_copies, part_copies):
        for copy in copies.values():
            copy.wait_send()


def kernel_form(R, S, *arguments):
    pair_rep = arguments[0]
    ti, tk, C = pair_rep.shape
    so = ti // S
    vmem, dma = pltpu.VMEM, pltpu.SemaphoreType.DMA
    return pl.pallas_call(
        functools.partial(kernel, (R, S, ti, tk, C)),
        out_shape=jax.ShapeDtypeStruct((so, R * ti, C), BF16),
        in_specs=[pl.BlockSpec(memory_space=pl.ANY)] * 8,
        out_specs=pl.BlockSpec(memory_space=pltpu.VMEM),
        scratch_shapes=[vmem(a.shape, a.dtype) for a in arguments]
        + [
            vmem((ti * tk, C), F32),
            vmem((ti * tk, C), F32),
            vmem((R, tk, ti, C), BF16),
            vmem((S, so, tk, C), BF16),
            vmem((so, S * tk, C), F32),
            vmem((R, S, so, ti, C), BF16),
            vmem((R, S, so, ti, C), BF16),
            vmem((R, so, ti, C), F32),
            dma((9,)), dma((R,)), dma((R,)), dma((S,)), dma((S,)), dma((R, S)), dma((R, S)),
        ],
        compiler_params=pltpu.CompilerParams(
            collective_id=0, has_side_effects=True, vmem_limit_bytes=56 * 2**20
        ),
    )(*arguments)


def solution(mesh):
    R, S = mesh.shape["row"], mesh.shape["col"]

    def on_device(*arguments):
        ti, tk, C = arguments[0].shape
        small = (
            R in (2, 4) and S in (2, 4) and R * ti == S * tk and C == 128
            and ti == 16 and tk == 16
        )
        if small:
            return kernel_form(R, S, *arguments)
        return general_form(*arguments)

    return jax.shard_map(
        on_device,
        mesh=mesh,
        in_specs=(P(("cplx", "row"), "col", None), P(("cplx", "row"), "col"))
        + (P(),) * 6,
        out_specs=P(("cplx", "row", "col"), None, None),
        check_vma=False,
    )
```
